32 devices in a mesh: serve: 2 (over x), store: 16 (over z, y, core).
Axes of the slice: x: 2, y: 2, z: 4, core: 2. Of those that a mesh axis runs over, the one named last changes fastest.
Arguments:
- normalized_hidden_states: bfloat16 [16384, 2048], P(('serve', 'store')), may hold values from -20 to 20
- query_weight_matrix: bfloat16 [2048, 2048], replicated, may hold values from -0.125 to 0.125
- key_weight_matrix: bfloat16 [2048, 512], replicated, may hold values from -0.125 to 0.125
- value_weight_matrix: bfloat16 [2048, 512], replicated, may hold values from -0.125 to 0.125
- adapter_down_weight: bfloat16 [512, 32, 2048], P('store', None, 'serve'), may hold values from -0.125 to 0.125
- adapter_up_query_weight: bfloat16 [512, 16, 2048], P('store', None, 'serve'), may hold values from -1.5 to 1.5
- adapter_up_value_weight: bfloat16 [512, 16, 512], P('store', None, 'serve'), may hold values from -1.5 to 1.5
- adapter_panel_slot: int32 [512], replicated, may hold values from 0 to 511, as said below
- adapter_per_request: int32 [32, 16], P(('serve', 'store')), may hold values from 0 to 511, as said below
- request_token_length: int32 [32, 16], P(('serve', 'store')), may hold values from 1 to 64, 512 in all within a row
Outputs:
- attended: bfloat16 [16384, 2048], P(('serve', 'store'))
The draws below stay inside these ranges and needn't reach their ends.
Inputs may be any that keep to these rules, and one draw needn't show every extreme that they name: Each number appears once; adapter a's panels are entry adapter_panel_slot[a] of the three panel arrays, whose owner is index adapter_panel_slot[a] // 32 of store. `adapter_per_request`: the 16 requests of one device use adapters of 16 different owners. `request_token_length`: each row sums to 512; the longest request of each device has exactly 64 tokens.
All inputs are finite; a program needn't handle non-finite values.
Results may differ from the reference program's by a relative error of at most 0.012.
Values may be sent and summed in bfloat16 or wider, within the bound.
A program may use at most 128 MiB of HBM per device.

```python
import math
import jax
import jax.numpy as jnp
import numpy as np
from jax import lax

MODEL_WIDTH = 2048
HEADS = 32
KV_HEADS = 8
HEAD_DIM = 64
ADAPTER_RANK = 16
ADP_DEV = 32
TOK_DEV = 512
KEY_VALUE_WIDTH = 512
LEN_MAX = 64
REQ_DEV = 16
ADAPTER_TOTAL = 512
TOKENS = 16384
N_SERVE = 2
N_STORE = 16


def shared_layout(key):
    return jax.random.permutation(jax.random.fold_in(key, 7), ADAPTER_TOTAL).astype(jnp.int32)


def draw_adapter_panel_slot(key, part):
    return shared_layout(key)


def draw_adapter_per_request(key, part):
    shuffled = shared_layout(key)
    inverse = jnp.argsort(shuffled, stable=True).astype(jnp.int32)
    row_count = N_SERVE * N_STORE
    scores = jax.random.randint(jax.random.fold_in(key, 13), (row_count, REQ_DEV), 0, 1 << 20) * REQ_DEV + jnp.arange(REQ_DEV, dtype=jnp.int32)[None, :]
    owners = jnp.argsort(scores, axis=1, stable=True).astype(jnp.int32)
    first_pick = jax.random.randint(jax.random.fold_in(key, 17), (row_count, REQ_DEV), 0, ADP_DEV)
    second_pick = jax.random.randint(jax.random.fold_in(key, 19), (row_count, REQ_DEV), 0, ADP_DEV)
    popular = jnp.minimum(first_pick, second_pick)
    slot_index_list = owners * ADP_DEV + popular
    return inverse[slot_index_list].astype(jnp.int32)


def draw_normalized_hidden_states(key, part):
    values = jnp.clip(jax.random.normal(jax.random.fold_in(key, 3), (TOKENS, MODEL_WIDTH)), -4.0, 4.0)
    return values.astype(jnp.float32).astype(jnp.bfloat16)


def steps_of(rng, shape, cuts, low, largest):
    def one(position, blocks):
        steps = jax.random.uniform(jax.random.fold_in(jax.random.fold_in(rng, 6), position), (blocks,), jnp.float32, low / len(cuts), largest / len(cuts))
        return jnp.repeat(jnp.exp(steps), shape[position] // blocks).reshape((-1,) + (1,) * (len(shape) - position - 1))

    factor_of = one(*cuts[0])
    for cut in cuts[1:]:
        factor_of = factor_of * one(*cut)
    return factor_of


def split_up(number_of, total, limit, slope):
    loads = [(1 << 20) // math.isqrt(rank ** slope) + 1 for rank in range(2, number_of + 1)]
    surplus, counts = total - limit - (number_of - 1), [1] * (number_of - 1)
    while surplus > 0:
        movable = [i for i in range(number_of - 1) if counts[i] < limit]
        pool, left = sum([loads[i] for i in movable]), surplus
        for i in movable:
            addition = min(limit - counts[i], max(1, left * loads[i] // pool), surplus)
            counts[i] = counts[i] + addition
            surplus = surplus - addition
    return np.array([limit] + counts)


def uneven(own_key, number_of, total, limit, slope):
    if number_of == 2:
        one = jax.random.randint(own_key, (), max(1, total - limit), min(limit, total - 1) + 1)
        return jnp.stack([one, total - one])
    tallies = jnp.asarray(split_up(number_of, total, limit, slope), jnp.int32)
    twos = (number_of - 1) // 2
    source_of, taker = tallies[1:1 + 2 * twos:2], tallies[2:2 + 2 * twos:2]
    room = jnp.minimum(source_of - 1, limit - taker)
    passed = jax.random.randint(jax.random.fold_in(own_key, 1), (twos,), 0, 1 << 20) % (room + 1)
    tallies = tallies.at[1:1 + 2 * twos:2].set(source_of - passed).at[2:2 + 2 * twos:2].set(taker + passed)
    return tallies[jax.random.permutation(jax.random.fold_in(own_key, 2), number_of)]


def noise(key, extent, spread, bound, cuts=(), held_as=jnp.bfloat16):
    entries = spread * jax.random.normal(key, extent, jnp.float32)
    if cuts:
        entries = entries * steps_of(key, extent, cuts, -0.22, 0.18)
    return jnp.clip(entries, -bound, bound).astype(held_as)


def setup_inputs(seed: int = 0) -> dict:
    key_of = jax.random.split(jax.random.key(seed), 11)
    normalized_hidden_states = draw_normalized_hidden_states(jax.random.fold_in(key_of[10], 71), 0)
    query_weight_matrix = noise(key_of[1], (MODEL_WIDTH, MODEL_WIDTH), MODEL_WIDTH ** -0.5, 0.125)
    key_weight_matrix = noise(key_of[2], (MODEL_WIDTH, KEY_VALUE_WIDTH), MODEL_WIDTH ** -0.5, 0.125)
    value_weight_matrix = noise(key_of[3], (MODEL_WIDTH, KEY_VALUE_WIDTH), MODEL_WIDTH ** -0.5, 0.125)
    adapter_down_weight = noise(key_of[4], (ADAPTER_TOTAL, 2 * ADAPTER_RANK, MODEL_WIDTH), MODEL_WIDTH ** -0.5, 0.125, ((0, 16), (2, 2)))
    adapter_up_query_weight = noise(key_of[5], (ADAPTER_TOTAL, ADAPTER_RANK, MODEL_WIDTH), ADAPTER_RANK ** -0.5, 1.5, ((0, 16), (2, 2)))
    adapter_up_value_weight = noise(key_of[6], (ADAPTER_TOTAL, ADAPTER_RANK, KEY_VALUE_WIDTH), ADAPTER_RANK ** -0.5, 1.5, ((0, 16), (2, 2)))
    adapter_panel_slot = draw_adapter_panel_slot(jax.random.fold_in(key_of[10], 71), 0)
    adapter_per_request = draw_adapter_per_request(jax.random.fold_in(key_of[10], 71), 0)
    request_token_length = jax.vmap(lambda own: uneven(own, REQ_DEV, TOK_DEV, LEN_MAX, 2))(jax.random.split(key_of[9], (N_SERVE * N_STORE))).reshape((N_SERVE * N_STORE, REQ_DEV)).astype(jnp.int32)
    return dict(normalized_hidden_states=normalized_hidden_states, query_weight_matrix=query_weight_matrix, key_weight_matrix=key_weight_matrix, value_weight_matrix=value_weight_matrix, adapter_down_weight=adapter_down_weight, adapter_up_query_weight=adapter_up_query_weight, adapter_up_value_weight=adapter_up_value_weight, adapter_panel_slot=adapter_panel_slot, adapter_per_request=adapter_per_request, request_token_length=request_token_length)


def rotary(heads_in, positions):
    half_dim = HEAD_DIM // 2
    frequency = 500000.0 ** (-(jnp.arange(half_dim).astype(jnp.float32) * 2.0 / HEAD_DIM))
    angles = positions.astype(jnp.float32)[:, None] * frequency[None, :]
    cosine_table = jnp.cos(angles)[:, None, :]
    sine_table = jnp.sin(angles)[:, None, :]
    first_half = heads_in[..., :half_dim]
    second_half = heads_in[..., half_dim:]
    return jnp.concatenate([first_half * cosine_table - second_half * sine_table,
                            second_half * cosine_table + first_half * sine_table], axis=-1)


def reduced_rank_products(block_list, down_panels, up_query, up_value):
    low = jnp.einsum('jkd,jrd->jkr', block_list.astype(jnp.float32), down_panels.astype(jnp.float32)).astype(jnp.bfloat16)
    query_update = jnp.einsum('jkr,jrd->jkd', low[..., :ADAPTER_RANK].astype(jnp.float32), up_query.astype(jnp.float32)).astype(jnp.bfloat16)
    value_update = jnp.einsum('jkr,jrd->jkd', low[..., ADAPTER_RANK:].astype(jnp.float32), up_value.astype(jnp.float32)).astype(jnp.bfloat16)
    return query_update, value_update


def attention(query_rot, key_rot, value_rows, request_ids):
    tok_rows = query_rot.shape[0]
    per_group = HEADS // KV_HEADS
    token_order = jnp.arange(tok_rows)
    allowed = (request_ids[:, None] == request_ids[None, :]) & (token_order[None, :] <= token_order[:, None])
    pieces = []
    for group_index in range(KV_HEADS):
        query_part = query_rot[:, group_index * per_group:(group_index + 1) * per_group, :].astype(jnp.float32)
        key_part = key_rot[:, group_index, :].astype(jnp.float32)
        value_part = value_rows[:, group_index, :].astype(jnp.float32)
        scores = jnp.einsum('qhd,kd->hqk', query_part, key_part) * (HEAD_DIM ** -0.5)
        scores = jnp.where(allowed[None], scores, -jnp.inf)
        row_max = jnp.max(scores, axis=-1, keepdims=True)
        raised = jnp.exp(scores - row_max)
        row_total = jnp.sum(raised, axis=-1)
        weights = raised.astype(jnp.bfloat16)
        mixed_heads = jnp.einsum('hqk,kd->qhd', weights.astype(jnp.float32), value_part) / jnp.transpose(row_total)[:, :, None]
        pieces.append(mixed_heads)
    return jnp.concatenate(pieces, axis=1).reshape(tok_rows, HEADS * HEAD_DIM).astype(jnp.bfloat16)


def reference(normalized_hidden_states, query_weight_matrix, key_weight_matrix, value_weight_matrix, adapter_down_weight, adapter_up_query_weight, adapter_up_value_weight, adapter_panel_slot, adapter_per_request, request_token_length):
    device_count = request_token_length.shape[0]
    tok_dev = normalized_hidden_states.shape[0] // device_count
    states = normalized_hidden_states.reshape(device_count, tok_dev, MODEL_WIDTH)

    def one_device(operands):
        states_dev, lengths, adapters = operands
        request_ends = jnp.cumsum(lengths).astype(jnp.int32)
        starts = (request_ends - lengths).astype(jnp.int32)
        token_order = jnp.arange(tok_dev, dtype=jnp.int32)
        request_ids = jnp.sum((token_order[:, None] >= request_ends[None, :]).astype(jnp.int32), axis=1).astype(jnp.int32)
        positions = (token_order - starts[request_ids]).astype(jnp.int32)
        offsets = jnp.arange(LEN_MAX, dtype=jnp.int32)
        valid_rows = offsets[None, :] < lengths[:, None]
        row_index = jnp.where(valid_rows, starts[:, None] + offsets[None, :], 0).astype(jnp.int32)
        block_list = jnp.where(valid_rows[..., None], states_dev[row_index], jnp.zeros((), jnp.bfloat16))
        slot_index_list = adapter_panel_slot[adapters]
        query_update, value_update = reduced_rank_products(block_list, adapter_down_weight[slot_index_list], adapter_up_query_weight[slot_index_list], adapter_up_value_weight[slot_index_list])
        delta_query = query_update[request_ids, positions]
        delta_value = value_update[request_ids, positions]
        base_query = jnp.dot(states_dev, query_weight_matrix, preferred_element_type=jnp.float32) + delta_query.astype(jnp.float32)
        query_rot = rotary(base_query.reshape(tok_dev, HEADS, HEAD_DIM), positions).astype(jnp.bfloat16)
        base_key = jnp.dot(states_dev, key_weight_matrix, preferred_element_type=jnp.float32)
        key_rot = rotary(base_key.reshape(tok_dev, KV_HEADS, HEAD_DIM), positions).astype(jnp.bfloat16)
        value_rows = (jnp.dot(states_dev, value_weight_matrix, preferred_element_type=jnp.float32) + delta_value.astype(jnp.float32)).astype(jnp.bfloat16)
        value_rows = value_rows.reshape(tok_dev, KV_HEADS, HEAD_DIM)
        return attention(query_rot, key_rot, value_rows, request_ids)

    result = lax.map(one_device, (states, request_token_length, adapter_per_request))
    return result.reshape(device_count * tok_dev, MODEL_WIDTH)
```

```python
import jax
import jax.numpy as jnp
from jax import lax
from jax.experimental import pallas as pl
from jax.experimental.pallas import tpu as pltpu
from jax.sharding import PartitionSpec as P

HEADS = 32
KV_HEADS = 8
HEAD_DIM = 64
RANK = 16
BLOCK = 64
LANES = 128
VMEM = pl.BlockSpec(memory_space=pltpu.VMEM)
CONTRACT_LAST = (((1,), (1,)), ((), ()))


def choose_kernel(pick_ref, down_ref, upq_ref, upv_ref, dsend_ref, qsend_ref, vsend_ref, sems):
    copies = []
    for dest in range(dsend_ref.shape[0]):
        entry = pick_ref[dest]
        copies.append(
            pltpu.make_async_copy(down_ref.at[entry], dsend_ref.at[dest], sems.at[0, dest])
        )
        copies.append(pltpu.make_async_copy(upq_ref.at[entry], qsend_ref.at[dest], sems.at[1, dest]))
        copies.append(pltpu.make_async_copy(upv_ref.at[entry], vsend_ref.at[dest], sems.at[2, dest]))
        for copy in copies[-3:]:
            copy.start()
    for copy in copies:
        copy.wait()


def choose(pick, down, upq, upv):
    count = pick.shape[0]
    anywhere = pl.BlockSpec(memory_space=pl.ANY)
    return pl.pallas_call(
        choose_kernel,
        out_shape=[
            jax.ShapeDtypeStruct((count,) + p.shape[1:], p.dtype) for p in (down, upq, upv)
        ],
        in_specs=[pl.BlockSpec(memory_space=pltpu.SMEM)] + [anywhere] * 3,
        out_specs=[anywhere] * 3,
        scratch_shapes=[pltpu.SemaphoreType.DMA((3, count))],
        name="choose",
    )(pick, down, upq, upv)


def low_kernel(x_ref, down_ref, owner_ref, lowq_ref, lowv_ref):
    serves, stores, _, _, width = down_ref.shape
    rows = x_ref.shape[0]
    cols = stores * RANK
    mine = owner_ref[:, :1] == lax.broadcasted_iota(jnp.int32, (rows, cols), 1) // RANK
    for part, out_ref in enumerate((lowq_ref, lowv_ref)):
        total = jnp.zeros((rows, cols), jnp.float32)
        for s in range(serves):
            total += lax.dot_general(
                x_ref[:, s * width : (s + 1) * width],
                down_ref[s, :, part].reshape(cols, width),
                CONTRACT_LAST,
                preferred_element_type=jnp.float32,
            )
        out_ref[...] = jnp.where(mine, total, 0.0).astype(jnp.bfloat16)


def low_products(x, down, owner):
    rows = x.shape[0]
    cols = down.shape[1] * RANK
    return pl.pallas_call(
        low_kernel,
        out_shape=[jax.ShapeDtypeStruct((rows, cols), jnp.bfloat16)] * 2,
        in_specs=[VMEM] * 3,
        out_specs=[VMEM] * 2,
        compiler_params=pltpu.CompilerParams(vmem_limit_bytes=32 << 20),
        name="low",
    )(x, down, owner)


def turned(x, cos, sin):
    lane = lax.broadcasted_iota(jnp.int32, x.shape, 1)
    other = jnp.where(
        lane % HEAD_DIM < HEAD_DIM // 2,
        pltpu.roll(x, LANES - HEAD_DIM // 2, 1),
        pltpu.roll(x, HEAD_DIM // 2, 1),
    )
    return x * cos + other * sin


def columns(ref):
    pieces, stores, rank, width = ref.shape
    parts = [ref[s].reshape(stores * rank, width) for s in range(pieces)]
    return parts[0] if pieces == 1 else jnp.concatenate(parts, axis=1)


def attend_kernel(
    baseq_ref, basek_ref, basev_ref, lowq_ref, lowv_ref, upq_ref, upv_ref, cos_ref, sin_ref, pos_ref, out_ref
):
    rows = baseq_ref.shape[0]
    half = lax.broadcasted_iota(jnp.int32, (rows, LANES), 1) < HEAD_DIM
    cos, sin = cos_ref[...], sin_ref[...]
    delta_q = jnp.dot(lowq_ref[...], columns(upq_ref), preferred_element_type=jnp.float32)
    base = baseq_ref[...] + delta_q.astype(jnp.bfloat16).astype(jnp.float32)
    query = [
        (turned(base[:, p * LANES : (p + 1) * LANES], cos, sin) * HEAD_DIM**-0.5).astype(jnp.bfloat16)
        for p in range(4)
    ]
    keys = turned(basek_ref[...], cos, sin)
    delta_v = jnp.dot(lowv_ref[...], columns(upv_ref), preferred_element_type=jnp.float32)
    values = basev_ref[...] + delta_v.astype(jnp.bfloat16).astype(jnp.float32)

    def split(x):
        left, right = jnp.where(half, x, 0.0), jnp.where(half, 0.0, x)
        return [
            (left.astype(jnp.bfloat16), pltpu.roll(left, HEAD_DIM, 1).astype(jnp.bfloat16)),
            (pltpu.roll(right, HEAD_DIM, 1).astype(jnp.bfloat16), right.astype(jnp.bfloat16)),
        ]

    key_parts, value_parts = split(keys), split(values)
    window = 2 * BLOCK
    ones_half = lax.broadcasted_iota(jnp.int32, (2 * window, LANES), 1) < HEAD_DIM
    ones_top = lax.broadcasted_iota(jnp.int32, (2 * window, LANES), 0) < window
    ones = jnp.where(ones_half == ones_top, 1.0, 0.0).astype(jnp.bfloat16)
    row = lax.broadcasted_iota(jnp.int32, (BLOCK, window), 0)
    col = lax.broadcasted_iota(jnp.int32, (BLOCK, window), 1)
    for b in range(rows // BLOCK):
        first = b * BLOCK
        start = max(0, first - BLOCK)
        here = slice(first, first + BLOCK)
        seen = slice(start, start + window)
        token, key = row + first, col + start
        allowed = (key <= token) & (key >= token - pos_ref[here, :])
        allowed = jnp.concatenate([allowed.astype(jnp.float32)] * 2, axis=0) > 0.5
        for g in range(2):
            kk = jnp.concatenate([part[seen] for part in key_parts[g]], axis=0)
            vv = jnp.concatenate([part[seen] for part in value_parts[g]], axis=0)
            vv = jnp.concatenate([vv, ones], axis=1)
            qq = jnp.concatenate([query[2 * g][here], query[2 * g + 1][here]], axis=0)
            scores = lax.dot_general(qq, kk, CONTRACT_LAST, preferred_element_type=jnp.float32)
            raised = []
            for side in range(2):
                s = jnp.where(allowed, scores[:, side * window : (side + 1) * window], -jnp.inf)
                raised.append(jnp.exp(s - jnp.max(s, axis=1, keepdims=True)))
            weights = jnp.concatenate(raised, axis=1).astype(jnp.bfloat16)
            mixed = jnp.dot(weights, vv, preferred_element_type=jnp.float32)
            done = (mixed[:, :LANES] / mixed[:, LANES:]).astype(jnp.bfloat16)
            for p in range(2):
                at = (2 * g + p) * LANES
                out_ref[here, at : at + LANES] = done[p * BLOCK : (p + 1) * BLOCK]


def up_spec(up, cols):
    serves, stores, rank, width = up.shape
    if width >= cols:
        per = width // cols
        return pl.BlockSpec((1, stores, rank, cols), lambda j: (j // per, 0, 0, j % per))
    return pl.BlockSpec((cols // width, stores, rank, width), lambda j: (j, 0, 0, 0))


def attend(baseq, basek, basev, lowq, lowv, upq, upv, cos, sin, pos):
    rows, width = baseq.shape
    steps = basek.shape[1] // LANES
    wide = width // steps

    def block(cols):
        return pl.BlockSpec((rows, cols), lambda j: (0, j))

    def whole(a):
        return pl.BlockSpec(a.shape, lambda j: (0, 0))

    return pl.pallas_call(
        attend_kernel,
        out_shape=jax.ShapeDtypeStruct((rows, width), jnp.bfloat16),
        grid=(steps,),
        in_specs=[
            block(wide),
            block(LANES),
            block(LANES),
            whole(lowq),
            whole(lowv),
            up_spec(upq, wide),
            up_spec(upv, LANES),
            whole(cos),
            whole(sin),
            whole(pos),
        ],
        out_specs=block(wide),
        compiler_params=pltpu.CompilerParams(vmem_limit_bytes=48 << 20),
        name="attend",
    )(baseq, basek, basev, lowq, lowv, upq, upv, cos, sin, pos)


def local(x, wq, wk, wv, down, upq, upv, panel_slot, adapters, lengths):
    axes = ("serve", "store")
    serves, stores = lax.axis_size("serve"), lax.axis_size("store")
    my_store = lax.axis_index("store")
    rows = x.shape[0]
    per_store = down.shape[0]
    lengths, adapters = lengths[0], adapters[0]
    requests = lengths.shape[0]

    entries = jnp.arange(panel_slot.shape[0], dtype=jnp.int32)
    slots = jnp.sum(jnp.where(adapters[:, None] == entries[None, :], panel_slot[None, :], 0), axis=1)
    owners = slots // per_store
    store_ids = jnp.arange(stores, dtype=jnp.int32)
    asked = jnp.sum(
        jnp.where(owners[None, :] == store_ids[:, None], slots[None, :] % per_store, 0), axis=1
    )
    all_asked = lax.all_gather(asked[None, :], axes, axis=0, tiled=True)
    pick = jnp.sum(jnp.where(store_ids[None, :] == my_store, all_asked, 0), axis=1)
    down_send, upq_send, upv_send = choose(pick, down, upq, upv)

    def exchange(a):
        return lax.all_to_all(a, axes, split_axis=0, concat_axis=0, tiled=True)

    width = down.shape[2]
    down_got = exchange(down_send).reshape(serves, stores, 2, RANK, width)
    upq_got = exchange(upq_send).reshape(serves, stores, RANK, width)
    upv_got = exchange(upv_send).reshape(serves, stores, RANK, upv.shape[2])

    order = jnp.arange(requests, dtype=jnp.int32)
    ends = jnp.sum(jnp.where(order[None, :] <= order[:, None], lengths[None, :], 0), axis=1)
    token = jnp.arange(rows, dtype=jnp.int32)
    member = (token[:, None] < ends[None, :]) & (token[:, None] >= (ends - lengths)[None, :])
    positions = token - jnp.sum(jnp.where(member, (ends - lengths)[None, :], 0), axis=1)
    owner = jnp.sum(jnp.where(member, owners[None, :], 0), axis=1)
    frequency = 500000.0 ** (
        -(jnp.arange(HEAD_DIM // 2).astype(jnp.float32) * 2.0 / HEAD_DIM)
    )
    angles = positions.astype(jnp.float32)[:, None] * frequency[None, :]
    cos, sin = jnp.cos(angles), jnp.sin(angles)
    cos = jnp.concatenate([cos] * 4, axis=1)
    sin = jnp.concatenate([-sin, sin] * 2, axis=1)
    pos = jnp.broadcast_to(positions[:, None], (rows, LANES))
    owner = jnp.broadcast_to(owner[:, None], (rows, LANES))

    baseq = jnp.dot(x, wq, preferred_element_type=jnp.float32)
    basek = jnp.dot(x, wk, preferred_element_type=jnp.float32)
    basev = jnp.dot(x, wv, preferred_element_type=jnp.float32)
    lowq, lowv = low_products(x, down_got, owner)
    return attend(baseq, basek, basev, lowq, lowv, upq_got, upv_got, cos, sin, pos)


def solution(mesh):
    both = P(("serve", "store"), None)
    panel = P("store", None, "serve")
    return jax.shard_map(
        local,
        mesh=mesh,
        in_specs=(both, P(), P(), P(), panel, panel, panel, P(), both, both),
        out_specs=both,
        check_vma=False,
    )
```

```python
import functools

import jax
import jax.numpy as jnp
from jax import lax
from jax.experimental import pallas as pl
from jax.experimental.pallas import tpu as pltpu
from jax.sharding import PartitionSpec as P

HEADS = 32
KV_HEADS = 8
HEAD_DIM = 64
RANK = 16
BLOCK = 64
LANES = 128
VMEM = pl.BlockSpec(memory_space=pltpu.VMEM)
CONTRACT_LAST = (((1,), (1,)), ((), ()))


def ask_kernel(serves, stores, asked_ref, all_ref, send_sems, recv_sems):
    count = serves * stores
    me = lax.axis_index("serve") * stores + lax.axis_index("store")

    def peer(step):
        there = lax.rem(me + step, count)
        return (there // stores, lax.rem(there, stores))

    def copy(step):
        return pltpu.make_async_remote_copy(
            src_ref=asked_ref,
            dst_ref=all_ref.at[me],
            send_sem=send_sems.at[step],
            recv_sem=recv_sems.at[step],
            device_id=peer(step),
            device_id_type=pl.DeviceIdType.MESH,
        )

    barrier = pltpu.get_barrier_semaphore()

    @pl.loop(1, count)
    def _(step):
        pl.semaphore_signal(
            barrier, inc=1, device_id=peer(step), device_id_type=pl.DeviceIdType.MESH
        )

    pl.semaphore_wait(barrier, count - 1)

    @pl.loop(1, count)
    def _(step):
        copy(step).start()

    all_ref[me] = asked_ref[...]

    @pl.loop(1, count)
    def _(step):
        copy(step).wait()


def ask(asked, serves, stores):
    count = serves * stores
    return pl.pallas_call(
        functools.partial(ask_kernel, serves, stores),
        out_shape=jax.ShapeDtypeStruct((count,) + asked.shape, asked.dtype),
        in_specs=[VMEM],
        out_specs=VMEM,
        scratch_shapes=[pltpu.SemaphoreType.DMA((count,)), pltpu.SemaphoreType.DMA((count,))],
        compiler_params=pltpu.CompilerParams(collective_id=0, has_side_effects=True),
        name="ask",
    )(asked)


def choose_kernel(joined, pick_ref, down_ref, upq_ref, upv_ref, dsend_ref, *rest):
    qsend_ref, vsend_ref, sems = (rest[0], rest[0], rest[1]) if joined else rest
    width = upq_ref.shape[2]

    def copies(dest):
        entry = pick_ref[dest]
        if joined:
            q_to = qsend_ref.at[dest, :, pl.ds(0, width)]
            v_to = vsend_ref.at[dest, :, pl.ds(width, upv_ref.shape[2])]
        else:
            q_to, v_to = qsend_ref.at[dest], vsend_ref.at[dest]
        return (
            pltpu.make_async_copy(down_ref.at[entry], dsend_ref.at[dest], sems.at[0, dest]),
            pltpu.make_async_copy(upq_ref.at[entry], q_to, sems.at[1, dest]),
            pltpu.make_async_copy(upv_ref.at[entry], v_to, sems.at[2, dest]),
        )

    @pl.loop(0, dsend_ref.shape[0])
    def _(dest):
        for copy in copies(dest):
            copy.start()

    @pl.loop(0, dsend_ref.shape[0])
    def _(dest):
        for copy in copies(dest):
            copy.wait()


def choose(pick, down, upq, upv, joined):
    count = pick.shape[0]
    anywhere = pl.BlockSpec(memory_space=pl.ANY)
    shapes = [down.shape[1:], upq.shape[1:], upv.shape[1:]]
    if joined:
        shapes[1:] = [(upq.shape[1], upq.shape[2] + upv.shape[2])]
    return pl.pallas_call(
        functools.partial(choose_kernel, joined),
        out_shape=[jax.ShapeDtypeStruct((count,) + shape, down.dtype) for shape in shapes],
        in_specs=[pl.BlockSpec(memory_space=pltpu.SMEM)] + [anywhere] * 3,
        out_specs=[VMEM] * len(shapes),
        scratch_shapes=[pltpu.SemaphoreType.DMA((3, count))],
        compiler_params=pltpu.CompilerParams(vmem_limit_bytes=32 << 20),
        name="choose",
    )(pick, down, upq, upv)


def low_kernel(x_ref, down_ref, owner_ref, lowq_ref, lowv_ref):
    serves, stores, _, _, width = down_ref.shape
    rows = x_ref.shape[0]
    cols = stores * RANK
    mine = owner_ref[:, :1] == lax.broadcasted_iota(jnp.int32, (rows, cols), 1) // RANK
    for part, out_ref in enumerate((lowq_ref, lowv_ref)):
        total = jnp.zeros((rows, cols), jnp.float32)
        for s in range(serves):
            total += lax.dot_general(
                x_ref[:, s * width : (s + 1) * width],
                down_ref[s, :, part].reshape(cols, width),
                CONTRACT_LAST,
                preferred_element_type=jnp.float32,
            )
        out_ref[...] = jnp.where(mine, total, 0.0).astype(jnp.bfloat16)


def low_products(x, down, owner):
    rows = x.shape[0]
    cols = down.shape[1] * RANK
    return pl.pallas_call(
        low_kernel,
        out_shape=[jax.ShapeDtypeStruct((rows, cols), jnp.bfloat16)] * 2,
        in_specs=[VMEM] * 3,
        out_specs=[VMEM] * 2,
        compiler_params=pltpu.CompilerParams(vmem_limit_bytes=32 << 20),
        name="low",
    )(x, down, owner)


def turned(x, cos, sin):
    lane = lax.broadcasted_iota(jnp.int32, x.shape, 1)
    other = jnp.where(
        lane % HEAD_DIM < HEAD_DIM // 2,
        pltpu.roll(x, LANES - HEAD_DIM // 2, 1),
        pltpu.roll(x, HEAD_DIM // 2, 1),
    )
    return x * cos + other * sin


def columns(ref):
    pieces, stores, rank, width = ref.shape
    parts = [ref[s].reshape(stores * rank, width) for s in range(pieces)]
    return parts[0] if pieces == 1 else jnp.concatenate(parts, axis=1)


def attend_kernel(
    baseq_ref, basek_ref, basev_ref, lowq_ref, lowv_ref, upq_ref, upv_ref, cos_ref, sin_ref, pos_ref, out_ref
):
    rows = baseq_ref.shape[0]
    half = lax.broadcasted_iota(jnp.int32, (rows, LANES), 1) < HEAD_DIM
    cos, sin = cos_ref[...], sin_ref[...]
    delta_q = jnp.dot(lowq_ref[...], columns(upq_ref), preferred_element_type=jnp.float32)
    base = baseq_ref[...] + delta_q.astype(jnp.bfloat16).astype(jnp.float32)
    query = [
        (turned(base[:, p * LANES : (p + 1) * LANES], cos, sin) * HEAD_DIM**-0.5).astype(jnp.bfloat16)
        for p in range(4)
    ]
    keys = turned(basek_ref[...], cos, sin)
    delta_v = jnp.dot(lowv_ref[...], columns(upv_ref), preferred_element_type=jnp.float32)
    values = basev_ref[...] + delta_v.astype(jnp.bfloat16).astype(jnp.float32)

    def split(x):
        left, right = jnp.where(half, x, 0.0), jnp.where(half, 0.0, x)
        return [
            (left.astype(jnp.bfloat16), pltpu.roll(left, HEAD_DIM, 1).astype(jnp.bfloat16)),
            (pltpu.roll(right, HEAD_DIM, 1).astype(jnp.bfloat16), right.astype(jnp.bfloat16)),
        ]

    key_parts, value_parts = split(keys), split(values)
    window = 2 * BLOCK
    ones_half = lax.broadcasted_iota(jnp.int32, (2 * window, LANES), 1) < HEAD_DIM
    ones_top = lax.broadcasted_iota(jnp.int32, (2 * window, LANES), 0) < window
    ones = jnp.where(ones_half == ones_top, 1.0, 0.0).astype(jnp.bfloat16)
    row = lax.broadcasted_iota(jnp.int32, (BLOCK, window), 0)
    col = lax.broadcasted_iota(jnp.int32, (BLOCK, window), 1)
    for b in range(rows // BLOCK):
        first = b * BLOCK
        start = max(0, first - BLOCK)
        here = slice(first, first + BLOCK)
        seen = slice(start, start + window)
        token, key = row + first, col + start
        allowed = (key <= token) & (key >= token - pos_ref[here, :])
        allowed = jnp.concatenate([allowed.astype(jnp.float32)] * 2, axis=0) > 0.5
        for g in range(2):
            kk = jnp.concatenate([part[seen] for part in key_parts[g]], axis=0)
            vv = jnp.concatenate([part[seen] for part in value_parts[g]], axis=0)
            vv = jnp.concatenate([vv, ones], axis=1)
            qq = jnp.concatenate([query[2 * g][here], query[2 * g + 1][here]], axis=0)
            scores = lax.dot_general(qq, kk, CONTRACT_LAST, preferred_element_type=jnp.float32)
            raised = []
            for side in range(2):
                s = jnp.where(allowed, scores[:, side * window : (side + 1) * window], -jnp.inf)
                raised.append(jnp.exp(s - jnp.max(s, axis=1, keepdims=True)))
            weights = jnp.concatenate(raised, axis=1).astype(jnp.bfloat16)
            mixed = jnp.dot(weights, vv, preferred_element_type=jnp.float32)
            done = (mixed[:, :LANES] / mixed[:, LANES:]).astype(jnp.bfloat16)
            for p in range(2):
                at = (2 * g + p) * LANES
                out_ref[here, at : at + LANES] = done[p * BLOCK : (p + 1) * BLOCK]


def up_spec(up, width, skip, cols):
    _, stores, rank, _ = up.shape
    if width >= cols:
        per, off = width // cols, skip // cols
        return pl.BlockSpec((1, stores, rank, cols), lambda j: (j // per, 0, 0, off + j % per))
    return pl.BlockSpec((cols // width, stores, rank, width), lambda j: (j, 0, 0, 0))


def attend(baseq, basek, basev, lowq, lowv, upq, upv, cos, sin, pos, serves, joined):
    rows, width = baseq.shape
    steps = basek.shape[1] // LANES
    wide = width // steps

    def block(cols):
        return pl.BlockSpec((rows, cols), lambda j: (0, j))

    def whole(a):
        return pl.BlockSpec(a.shape, lambda j: (0, 0))

    return pl.pallas_call(
        attend_kernel,
        out_shape=jax.ShapeDtypeStruct((rows, width), jnp.bfloat16),
        grid=(steps,),
        in_specs=[
            block(wide),
            block(LANES),
            block(LANES),
            whole(lowq),
            whole(lowv),
            up_spec(upq, width // serves, 0, wide),
            up_spec(upv, basev.shape[1] // serves, width // serves if joined else 0, LANES),
            whole(cos),
            whole(sin),
            whole(pos),
        ],
        out_specs=block(wide),
        compiler_params=pltpu.CompilerParams(vmem_limit_bytes=48 << 20),
        name="attend",
    )(baseq, basek, basev, lowq, lowv, upq, upv, cos, sin, pos)


def local(x, wq, wk, wv, down, upq, upv, panel_slot, adapters, lengths):
    axes = ("serve", "store")
    serves, stores = lax.axis_size("serve"), lax.axis_size("store")
    my_store = lax.axis_index("store")
    rows = x.shape[0]
    per_store = down.shape[0]
    lengths, adapters = lengths[0], adapters[0]
    requests = lengths.shape[0]

    entries = jnp.arange(panel_slot.shape[0], dtype=jnp.int32)
    slots = jnp.sum(jnp.where(adapters[:, None] == entries[None, :], panel_slot[None, :], 0), axis=1)
    owners = slots // per_store
    store_ids = jnp.arange(stores, dtype=jnp.int32)
    asked = jnp.sum(
        jnp.where(owners[None, :] == store_ids[:, None], slots[None, :] % per_store, 0), axis=1
    )
    row = jnp.pad(asked, (0, LANES - stores))[None, :]
    all_asked = ask(row, serves, stores)[:, 0, :]
    lanes = jnp.arange(LANES, dtype=jnp.int32)
    pick = jnp.sum(jnp.where(lanes[None, :] == my_store, all_asked, 0), axis=1)
    joined = upv.shape[2] % LANES == 0

    def exchange(a):
        return lax.all_to_all(a, axes, split_axis=0, concat_axis=0, tiled=True)

    down_got, *up_got = [exchange(a) for a in choose(pick, down, upq, upv, joined)]
    down_got = down_got.reshape(serves, stores, 2, RANK, down.shape[2])
    up_got = [a.reshape((serves, stores) + a.shape[1:]) for a in up_got]
    upq_got, upv_got = up_got[0], up_got[-1]

    order = jnp.arange(requests, dtype=jnp.int32)
    ends = jnp.sum(jnp.where(order[None, :] <= order[:, None], lengths[None, :], 0), axis=1)
    token = jnp.arange(rows, dtype=jnp.int32)
    member = (token[:, None] < ends[None, :]) & (token[:, None] >= (ends - lengths)[None, :])
    positions = token - jnp.sum(jnp.where(member, (ends - lengths)[None, :], 0), axis=1)
    owner = jnp.sum(jnp.where(member, owners[None, :], 0), axis=1)
    frequency = 500000.0 ** (
        -(jnp.arange(HEAD_DIM // 2).astype(jnp.float32) * 2.0 / HEAD_DIM)
    )
    angles = positions.astype(jnp.float32)[:, None] * frequency[None, :]
    cos, sin = jnp.cos(angles), jnp.sin(angles)
    cos = jnp.concatenate([cos] * 4, axis=1)
    sin = jnp.concatenate([-sin, sin] * 2, axis=1)
    pos = jnp.broadcast_to(positions[:, None], (rows, LANES))
    owner = jnp.broadcast_to(owner[:, None], (rows, LANES))

    baseq = jnp.dot(x, wq, preferred_element_type=jnp.float32)
    basek = jnp.dot(x, wk, preferred_element_type=jnp.float32)
    basev = jnp.dot(x, wv, preferred_element_type=jnp.float32)
    lowq, lowv = low_products(x, down_got, owner)
    return attend(baseq, basek, basev, lowq, lowv, upq_got, upv_got, cos, sin, pos, serves, joined)


def solution(mesh):
    both = P(("serve", "store"), None)
    panel = P("store", None, "serve")
    return jax.shard_map(
        local,
        mesh=mesh,
        in_specs=(both, P(), P(), P(), panel, panel, panel, P(), both, both),
        out_specs=both,
        check_vma=False,
    )
```

```python
import functools

import jax
import jax.numpy as jnp
from jax import lax
from jax.experimental import pallas as pl
from jax.experimental.pallas import tpu as pltpu
from jax.sharding import PartitionSpec as P

HEADS = 32
KV_HEADS = 8
HEAD_DIM = 64
RANK = 16
BLOCK = 64
LANES = 128
VMEM = pl.BlockSpec(memory_space=pltpu.VMEM)
CONTRACT_LAST = (((1,), (1,)), ((), ()))


def ask_kernel(serves, stores, asked_ref, all_ref, send_sems, recv_sems):
    count = serves * stores
    me = lax.axis_index("serve") * stores + lax.axis_index("store")

    def peer(step):
        there = lax.rem(me + step, count)
        return (there // stores, lax.rem(there, stores))

    def copy(step):
        return pltpu.make_async_remote_copy(
            src_ref=asked_ref,
            dst_ref=all_ref.at[me],
            send_sem=send_sems.at[step],
            recv_sem=recv_sems.at[step],
            device_id=peer(step),
            device_id_type=pl.DeviceIdType.MESH,
        )

    barrier = pltpu.get_barrier_semaphore()

    @pl.loop(1, count)
    def _(step):
        pl.semaphore_signal(
            barrier, inc=1, device_id=peer(step), device_id_type=pl.DeviceIdType.MESH
        )

    pl.semaphore_wait(barrier, count - 1)

    @pl.loop(1, count)
    def _(step):
        copy(step).start()

    all_ref[me] = asked_ref[...]

    @pl.loop(1, count)
    def _(step):
        copy(step).wait()


def ask(asked, serves, stores):
    count = serves * stores
    return pl.pallas_call(
        functools.partial(ask_kernel, serves, stores),
        out_shape=jax.ShapeDtypeStruct((count,) + asked.shape, asked.dtype),
        in_specs=[VMEM],
        out_specs=VMEM,
        scratch_shapes=[pltpu.SemaphoreType.DMA((count,)), pltpu.SemaphoreType.DMA((count,))],
        compiler_params=pltpu.CompilerParams(collective_id=0, has_side_effects=True),
        name="ask",
    )(asked)


def choose_kernel(joined, pick_ref, down_ref, upq_ref, upv_ref, dsend_ref, *rest):
    qsend_ref, vsend_ref, sems = (rest[0], rest[0], rest[1]) if joined else rest
    width = upq_ref.shape[2]

    def copies(dest):
        entry = pick_ref[dest]
        if joined:
            q_to = qsend_ref.at[dest, :, pl.ds(0, width)]
            v_to = vsend_ref.at[dest, :, pl.ds(width, upv_ref.shape[2])]
        else:
            q_to, v_to = qsend_ref.at[dest], vsend_ref.at[dest]
        return (
            pltpu.make_async_copy(down_ref.at[entry], dsend_ref.at[dest], sems.at[0, dest]),
            pltpu.make_async_copy(upq_ref.at[entry], q_to, sems.at[1, dest]),
            pltpu.make_async_copy(upv_ref.at[entry], v_to, sems.at[2, dest]),
        )

    @pl.loop(0, dsend_ref.shape[0])
    def _(dest):
        for copy in copies(dest):
            copy.start()

    @pl.loop(0, dsend_ref.shape[0])
    def _(dest):
        for copy in copies(dest):
            copy.wait()


def choose(pick, down, upq, upv, joined):
    count = pick.shape[0]
    anywhere = pl.BlockSpec(memory_space=pl.ANY)
    shapes = [down.shape[1:], upq.shape[1:], upv.shape[1:]]
    if joined:
        shapes[1:] = [(upq.shape[1], upq.shape[2] + upv.shape[2])]
    return pl.pallas_call(
        functools.partial(choose_kernel, joined),
        out_shape=[jax.ShapeDtypeStruct((count,) + shape, down.dtype) for shape in shapes],
        in_specs=[pl.BlockSpec(memory_space=pltpu.SMEM)] + [anywhere] * 3,
        out_specs=[VMEM] * len(shapes),
        scratch_shapes=[pltpu.SemaphoreType.DMA((3, count))],
        compiler_params=pltpu.CompilerParams(vmem_limit_bytes=32 << 20),
        name="choose",
    )(pick, down, upq, upv)


def exchange_kernel(serves, stores, ups, *refs):
    owner_ref, x_hbm, wq_hbm, wk_hbm, wv_hbm, *refs = refs
    sends, refs = refs[: 1 + ups], refs[1 + ups :]
    baseq_hbm, basek_hbm, basev_hbm, lowq_ref, lowv_ref, *refs = refs
    ups_got, refs = refs[:ups], refs[ups:]
    down_got, x_ref, wq_ref, wk_ref, wv_ref, baseq_ref, basek_ref, basev_ref, *sems = refs
    send_sems, recv_sems, in_sems, out_sems = sems
    gots = [down_got] + list(ups_got)
    count = serves * stores
    me = lax.axis_index("serve") * stores + lax.axis_index("store")

    def peer(step):
        there = lax.rem(me + step, count)
        return there, (there // stores, lax.rem(there, stores))

    def copy(which, step):
        there, device = peer(step)
        return pltpu.make_async_remote_copy(
            src_ref=sends[which].at[there],
            dst_ref=gots[which].at[me],
            send_sem=send_sems.at[which, step],
            recv_sem=recv_sems.at[which, step],
            device_id=device,
            device_id_type=pl.DeviceIdType.MESH,
        )

    loads = [
        pltpu.make_async_copy(source, target, in_sems.at[i])
        for i, (source, target) in enumerate(
            [(x_hbm, x_ref), (wq_hbm, wq_ref), (wk_hbm, wk_ref), (wv_hbm, wv_ref)]
        )
    ]
    for load in loads:
        load.start()

    barrier = pltpu.get_barrier_semaphore()

    @pl.loop(1, count)
    def _(step):
        pl.semaphore_signal(
            barrier, inc=1, device_id=peer(step)[1], device_id_type=pl.DeviceIdType.MESH
        )

    pl.semaphore_wait(barrier, count - 1)

    for which in range(1 + ups):

        @pl.loop(1, count)
        def _(step):
            copy(which, step).start()

    for send, got in zip(sends, gots):
        got[me] = send[me]

    for load in loads:
        load.wait()
    stores_out = []
    for i, (w_ref, base_ref, base_hbm) in enumerate(
        [
            (wq_ref, baseq_ref, baseq_hbm),
            (wk_ref, basek_ref, basek_hbm),
            (wv_ref, basev_ref, basev_hbm),
        ]
    ):
        tile = min(256, w_ref.shape[1])

        @pl.loop(0, w_ref.shape[1] // tile)
        def _(c):
            at = pl.ds(pl.multiple_of(c * tile, tile), tile)
            base_ref[:, at] = jnp.dot(
                x_ref[...], w_ref[:, at], preferred_element_type=jnp.float32
            )

        stores_out.append(pltpu.make_async_copy(base_ref, base_hbm, out_sems.at[i]))
        stores_out[-1].start()

    @pl.loop(1, count)
    def _(step):
        copy(0, step).wait_recv()

    rows = x_ref.shape[0]
    width = down_got.shape[2]
    cols = stores * RANK
    mine = owner_ref[:, :1] == lax.broadcasted_iota(jnp.int32, (rows, cols), 1) // RANK
    for part, out_ref in enumerate((lowq_ref, lowv_ref)):
        total = jnp.zeros((rows, cols), jnp.float32)
        for s in range(serves):
            panels = down_got[s * stores : (s + 1) * stores, part * RANK : (part + 1) * RANK, :]
            total += lax.dot_general(
                x_ref[:, s * width : (s + 1) * width],
                panels.reshape(cols, width),
                CONTRACT_LAST,
                preferred_element_type=jnp.float32,
            )
        out_ref[...] = jnp.where(mine, total, 0.0).astype(jnp.bfloat16)

    for which in range(1, 1 + ups):

        @pl.loop(1, count)
        def _(step):
            copy(which, step).wait_recv()

    for which in range(1 + ups):

        @pl.loop(1, count)
        def _(step):
            copy(which, step).wait_send()

    for store in stores_out:
        store.wait()


def exchange(owner, x, weights, sends, serves, stores):
    count = serves * stores
    rows = x.shape[0]
    ups = len(sends) - 1
    anywhere = pl.BlockSpec(memory_space=pl.ANY)
    bases = [(rows, w.shape[1]) for w in weights]
    low = jax.ShapeDtypeStruct((rows, stores * RANK), jnp.bfloat16)
    return pl.pallas_call(
        functools.partial(exchange_kernel, serves, stores, ups),
        out_shape=[jax.ShapeDtypeStruct(base, jnp.float32) for base in bases]
        + [low, low]
        + [jax.ShapeDtypeStruct(a.shape, a.dtype) for a in sends[1:]],
        in_specs=[VMEM] + [anywhere] * 4 + [VMEM] * len(sends),
        out_specs=[anywhere] * 3 + [VMEM] * (2 + ups),
        scratch_shapes=[pltpu.VMEM(sends[0].shape, sends[0].dtype), pltpu.VMEM(x.shape, x.dtype)]
        + [pltpu.VMEM(w.shape, w.dtype) for w in weights]
        + [pltpu.VMEM(base, jnp.float32) for base in bases]
        + [
            pltpu.SemaphoreType.DMA((1 + ups, count)),
            pltpu.SemaphoreType.DMA((1 + ups, count)),
            pltpu.SemaphoreType.DMA((4,)),
            pltpu.SemaphoreType.DMA((3,)),
        ],
        compiler_params=pltpu.CompilerParams(
            collective_id=1, has_side_effects=True, vmem_limit_bytes=56 << 20
        ),
        name="exchange",
    )(owner, x, *weights, *sends)


def turned(x, cos, sin):
    lane = lax.broadcasted_iota(jnp.int32, x.shape, 1)
    other = jnp.where(
        lane % HEAD_DIM < HEAD_DIM // 2,
        pltpu.roll(x, LANES - HEAD_DIM // 2, 1),
        pltpu.roll(x, HEAD_DIM // 2, 1),
    )
    return x * cos + other * sin


def columns(ref):
    pieces, stores, rank, width = ref.shape
    parts = [ref[s].reshape(stores * rank, width) for s in range(pieces)]
    return parts[0] if pieces == 1 else jnp.concatenate(parts, axis=1)


def attend_kernel(
    baseq_ref, basek_ref, basev_ref, lowq_ref, lowv_ref, upq_ref, upv_ref, cos_ref, sin_ref, pos_ref, out_ref
):
    rows = baseq_ref.shape[0]
    half = lax.broadcasted_iota(jnp.int32, (rows, LANES), 1) < HEAD_DIM
    cos, sin = cos_ref[...], sin_ref[...]
    delta_q = jnp.dot(lowq_ref[...], columns(upq_ref), preferred_element_type=jnp.float32)
    base = baseq_ref[...] + delta_q.astype(jnp.bfloat16).astype(jnp.float32)
    query = [
        (turned(base[:, p * LANES : (p + 1) * LANES], cos, sin) * HEAD_DIM**-0.5).astype(jnp.bfloat16)
        for p in range(4)
    ]
    keys = turned(basek_ref[...], cos, sin)
    delta_v = jnp.dot(lowv_ref[...], columns(upv_ref), preferred_element_type=jnp.float32)
    values = basev_ref[...] + delta_v.astype(jnp.bfloat16).astype(jnp.float32)

    def split(x):
        left, right = jnp.where(half, x, 0.0), jnp.where(half, 0.0, x)
        return [
            (left.astype(jnp.bfloat16), pltpu.roll(left, HEAD_DIM, 1).astype(jnp.bfloat16)),
            (pltpu.roll(right, HEAD_DIM, 1).astype(jnp.bfloat16), right.astype(jnp.bfloat16)),
        ]

    key_parts, value_parts = split(keys), split(values)
    window = 2 * BLOCK
    ones_half = lax.broadcasted_iota(jnp.int32, (2 * window, LANES), 1) < HEAD_DIM
    ones_top = lax.broadcasted_iota(jnp.int32, (2 * window, LANES), 0) < window
    ones = jnp.where(ones_half == ones_top, 1.0, 0.0).astype(jnp.bfloat16)
    row = lax.broadcasted_iota(jnp.int32, (BLOCK, window), 0)
    col = lax.broadcasted_iota(jnp.int32, (BLOCK, window), 1)
    for b in range(rows // BLOCK):
        first = b * BLOCK
        start = max(0, first - BLOCK)
        here = slice(first, first + BLOCK)
        seen = slice(start, start + window)
        token, key = row + first, col + start
        allowed = (key <= token) & (key >= token - pos_ref[here, :])
        allowed = jnp.concatenate([allowed.astype(jnp.float32)] * 2, axis=0) > 0.5
        for g in range(2):
            kk = jnp.concatenate([part[seen] for part in key_parts[g]], axis=0)
            vv = jnp.concatenate([part[seen] for part in value_parts[g]], axis=0)
            vv = jnp.concatenate([vv, ones], axis=1)
            qq = jnp.concatenate([query[2 * g][here], query[2 * g + 1][here]], axis=0)
            scores = lax.dot_general(qq, kk, CONTRACT_LAST, preferred_element_type=jnp.float32)
            raised = []
            for side in range(2):
                s = jnp.where(allowed, scores[:, side * window : (side + 1) * window], -jnp.inf)
                raised.append(jnp.exp(s - jnp.max(s, axis=1, keepdims=True)))
            weights = jnp.concatenate(raised, axis=1).astype(jnp.bfloat16)
            mixed = jnp.dot(weights, vv, preferred_element_type=jnp.float32)
            done = (mixed[:, :LANES] / mixed[:, LANES:]).astype(jnp.bfloat16)
            for p in range(2):
                at = (2 * g + p) * LANES
                out_ref[here, at : at + LANES] = done[p * BLOCK : (p + 1) * BLOCK]


def up_spec(up, width, skip, cols):
    _, stores, rank, _ = up.shape
    if width >= cols:
        per, off = width // cols, skip // cols
        return pl.BlockSpec((1, stores, rank, cols), lambda j: (j // per, 0, 0, off + j % per))
    return pl.BlockSpec((cols // width, stores, rank, width), lambda j: (j, 0, 0, 0))


def attend(baseq, basek, basev, lowq, lowv, upq, upv, cos, sin, pos, serves, joined):
    rows, width = baseq.shape
    steps = basek.shape[1] // LANES
    wide = width // steps

    def block(cols):
        return pl.BlockSpec((rows, cols), lambda j: (0, j))

    def whole(a):
        return pl.BlockSpec(a.shape, lambda j: (0, 0))

    return pl.pallas_call(
        attend_kernel,
        out_shape=jax.ShapeDtypeStruct((rows, width), jnp.bfloat16),
        grid=(steps,),
        in_specs=[
            block(wide),
            block(LANES),
            block(LANES),
            whole(lowq),
            whole(lowv),
            up_spec(upq, width // serves, 0, wide),
            up_spec(upv, basev.shape[1] // serves, width // serves if joined else 0, LANES),
            whole(cos),
            whole(sin),
            whole(pos),
        ],
        out_specs=block(wide),
        compiler_params=pltpu.CompilerParams(vmem_limit_bytes=60 << 20),
        name="attend",
    )(baseq, basek, basev, lowq, lowv, upq, upv, cos, sin, pos)


def local(x, wq, wk, wv, down, upq, upv, panel_slot, adapters, lengths):
    axes = ("serve", "store")
    serves, stores = lax.axis_size("serve"), lax.axis_size("store")
    my_store = lax.axis_index("store")
    rows = x.shape[0]
    per_store = down.shape[0]
    lengths, adapters = lengths[0], adapters[0]
    requests = lengths.shape[0]

    entries = jnp.arange(panel_slot.shape[0], dtype=jnp.int32)
    slots = jnp.sum(jnp.where(adapters[:, None] == entries[None, :], panel_slot[None, :], 0), axis=1)
    owners = slots // per_store
    store_ids = jnp.arange(stores, dtype=jnp.int32)
    asked = jnp.sum(
        jnp.where(owners[None, :] == store_ids[:, None], slots[None, :] % per_store, 0), axis=1
    )
    row = jnp.pad(asked, (0, LANES - stores))[None, :]
    all_asked = ask(row, serves, stores)[:, 0, :]
    lanes = jnp.arange(LANES, dtype=jnp.int32)
    pick = jnp.sum(jnp.where(lanes[None, :] == my_store, all_asked, 0), axis=1)
    joined = upv.shape[2] % LANES == 0

    sends = choose(pick, down, upq, upv, joined)

    order = jnp.arange(requests, dtype=jnp.int32)
    ends = jnp.sum(jnp.where(order[None, :] <= order[:, None], lengths[None, :], 0), axis=1)
    token = jnp.arange(rows, dtype=jnp.int32)
    member = (token[:, None] < ends[None, :]) & (token[:, None] >= (ends - lengths)[None, :])
    positions = token - jnp.sum(jnp.where(member, (ends - lengths)[None, :], 0), axis=1)
    owner = jnp.sum(jnp.where(member, owners[None, :], 0), axis=1)
    frequency = 500000.0 ** (
        -(jnp.arange(HEAD_DIM // 2).astype(jnp.float32) * 2.0 / HEAD_DIM)
    )
    angles = positions.astype(jnp.float32)[:, None] * frequency[None, :]
    cos, sin = jnp.cos(angles), jnp.sin(angles)
    cos = jnp.concatenate([cos] * 4, axis=1)
    sin = jnp.concatenate([-sin, sin] * 2, axis=1)
    pos = jnp.broadcast_to(positions[:, None], (rows, LANES))
    owner = jnp.broadcast_to(owner[:, None], (rows, LANES))

    baseq, basek, basev, lowq, lowv, *up_got = exchange(
        owner, x, (wq, wk, wv), sends, serves, stores
    )
    up_got = [a.reshape((serves, stores) + a.shape[1:]) for a in up_got]
    upq_got, upv_got = up_got[0], up_got[-1]
    return attend(baseq, basek, basev, lowq, lowv, upq_got, upv_got, cos, sin, pos, serves, joined)


def solution(mesh):
    both = P(("serve", "store"), None)
    panel = P("store", None, "serve")
    return jax.shard_map(
        local,
        mesh=mesh,
        in_specs=(both, P(), P(), P(), panel, panel, panel, P(), both, both),
        out_specs=both,
        check_vma=False,
    )
```

```python
import functools

import jax
import jax.numpy as jnp
from jax import lax
from jax.experimental import pallas as pl
from jax.experimental.pallas import tpu as pltpu
from jax.sharding import PartitionSpec as P

HEADS = 32
KV_HEADS = 8
HEAD_DIM = 64
RANK = 16
BLOCK = 64
LANES = 128
VMEM = pl.BlockSpec(memory_space=pltpu.VMEM)
CONTRACT_LAST = (((1,), (1,)), ((), ()))


def ask_kernel(serves, stores, asked_ref, all_ref, send_sems, recv_sems):
    count = serves * stores
    me = lax.axis_index("serve") * stores + lax.axis_index("store")

    def peer(step):
        there = lax.rem(me + step, count)
        return (there // stores, lax.rem(there, stores))

    def copy(step):
        return pltpu.make_async_remote_copy(
            src_ref=asked_ref,
            dst_ref=all_ref.at[me],
            send_sem=send_sems.at[step],
            recv_sem=recv_sems.at[step],
            device_id=peer(step),
            device_id_type=pl.DeviceIdType.MESH,
        )

    barrier = pltpu.get_barrier_semaphore()

    @pl.loop(1, count)
    def _(step):
        pl.semaphore_signal(
            barrier, inc=1, device_id=peer(step), device_id_type=pl.DeviceIdType.MESH
        )

    pl.semaphore_wait(barrier, count - 1)

    @pl.loop(1, count)
    def _(step):
        copy(step).start()

    all_ref[me] = asked_ref[...]

    @pl.loop(1, count)
    def _(step):
        copy(step).wait()


def ask(asked, serves, stores):
    count = serves * stores
    return pl.pallas_call(
        functools.partial(ask_kernel, serves, stores),
        out_shape=jax.ShapeDtypeStruct((count,) + asked.shape, asked.dtype),
        in_specs=[VMEM],
        out_specs=VMEM,
        scratch_shapes=[pltpu.SemaphoreType.DMA((count,)), pltpu.SemaphoreType.DMA((count,))],
        compiler_params=pltpu.CompilerParams(collective_id=0, has_side_effects=True),
        name="ask",
    )(asked)


def choose_kernel(joined, pick_ref, down_ref, upq_ref, upv_ref, dsend_ref, *rest):
    qsend_ref, vsend_ref, sems = (rest[0], rest[0], rest[1]) if joined else rest
    width = upq_ref.shape[2]

    def copies(dest):
        entry = pick_ref[dest]
        if joined:
            q_to = qsend_ref.at[dest, :, pl.ds(0, width)]
            v_to = vsend_ref.at[dest, :, pl.ds(width, upv_ref.shape[2])]
        else:
            q_to, v_to = qsend_ref.at[dest], vsend_ref.at[dest]
        return (
            pltpu.make_async_copy(down_ref.at[entry], dsend_ref.at[dest], sems.at[0, dest]),
            pltpu.make_async_copy(upq_ref.at[entry], q_to, sems.at[1, dest]),
            pltpu.make_async_copy(upv_ref.at[entry], v_to, sems.at[2, dest]),
        )

    @pl.loop(0, dsend_ref.shape[0])
    def _(dest):
        for copy in copies(dest):
            copy.start()

    @pl.loop(0, dsend_ref.shape[0])
    def _(dest):
        for copy in copies(dest):
            copy.wait()


def choose(pick, down, upq, upv, joined):
    count = pick.shape[0]
    anywhere = pl.BlockSpec(memory_space=pl.ANY)
    shapes = [down.shape[1:], upq.shape[1:], upv.shape[1:]]
    if joined:
        shapes[1:] = [(upq.shape[1], upq.shape[2] + upv.shape[2])]
    return pl.pallas_call(
        functools.partial(choose_kernel, joined),
        out_shape=[jax.ShapeDtypeStruct((count,) + shape, down.dtype) for shape in shapes],
        in_specs=[pl.BlockSpec(memory_space=pltpu.SMEM)] + [anywhere] * 3,
        out_specs=[VMEM] * len(shapes),
        scratch_shapes=[pltpu.SemaphoreType.DMA((3, count))],
        compiler_params=pltpu.CompilerParams(vmem_limit_bytes=60 << 20),
        name="choose",
    )(pick, down, upq, upv)


def exchange_kernel(serves, stores, ups, *refs):
    owner_ref, x_hbm, wq_hbm, wk_hbm, wv_hbm, *refs = refs
    sends, refs = refs[: 1 + ups], refs[1 + ups :]
    baseq_hbm, basek_hbm, basev_hbm, lowq_ref, lowv_ref, *refs = refs
    ups_got, refs = refs[:ups], refs[ups:]
    down_got, x_ref, wq_ref, wk_ref, wv_ref, baseq_ref, basek_ref, basev_ref, *sems = refs
    send_sems, recv_sems, in_sems, out_sems = sems
    gots = [down_got] + list(ups_got)
    count = serves * stores
    me = lax.axis_index("serve") * stores + lax.axis_index("store")

    def peer(step):
        there = lax.rem(me + step, count)
        return there, (there // stores, lax.rem(there, stores))

    def copy(which, step):
        there, device = peer(step)
        return pltpu.make_async_remote_copy(
            src_ref=sends[which].at[there],
            dst_ref=gots[which].at[me],
            send_sem=send_sems.at[which, step],
            recv_sem=recv_sems.at[which, step],
            device_id=device,
            device_id_type=pl.DeviceIdType.MESH,
        )

    loads = [
        pltpu.make_async_copy(source, target, in_sems.at[i])
        for i, (source, target) in enumerate(
            [(x_hbm, x_ref), (wq_hbm, wq_ref), (wk_hbm, wk_ref), (wv_hbm, wv_ref)]
        )
    ]
    for load in loads:
        load.start()

    barrier = pltpu.get_barrier_semaphore()

    @pl.loop(1, count)
    def _(step):
        pl.semaphore_signal(
            barrier, inc=1, device_id=peer(step)[1], device_id_type=pl.DeviceIdType.MESH
        )

    pl.semaphore_wait(barrier, count - 1)

    for which in range(1 + ups):

        @pl.loop(1, count)
        def _(step):
            copy(which, step).start()

    for send, got in zip(sends, gots):
        got[me] = send[me]

    for load in loads:
        load.wait()
    stores_out = []
    for i, (w_ref, base_ref, base_hbm) in enumerate(
        [
            (wq_ref, baseq_ref, baseq_hbm),
            (wk_ref, basek_ref, basek_hbm),
            (wv_ref, basev_ref, basev_hbm),
        ]
    ):
        tile = min(256, w_ref.shape[1])

        @pl.loop(0, w_ref.shape[1] // tile)
        def _(c):
            at = pl.ds(pl.multiple_of(c * tile, tile), tile)
            base_ref[:, at] = jnp.dot(
                x_ref[...], w_ref[:, at], preferred_element_type=jnp.float32
            )

        stores_out.append(pltpu.make_async_copy(base_ref, base_hbm, out_sems.at[i]))
        stores_out[-1].start()

    @pl.loop(1, count)
    def _(step):
        copy(0, step).wait_recv()

    rows = x_ref.shape[0]
    width = down_got.shape[2]
    cols = stores * RANK
    mine = owner_ref[:, :1] == lax.broadcasted_iota(jnp.int32, (rows, cols), 1) // RANK
    for part, out_ref in enumerate((lowq_ref, lowv_ref)):
        total = jnp.zeros((rows, cols), jnp.float32)
        for s in range(serves):
            panels = down_got[s * stores : (s + 1) * stores, part * RANK : (part + 1) * RANK, :]
            total += lax.dot_general(
                x_ref[:, s * width : (s + 1) * width],
                panels.reshape(cols, width),
                CONTRACT_LAST,
                preferred_element_type=jnp.float32,
            )
        out_ref[...] = jnp.where(mine, total, 0.0).astype(jnp.bfloat16)

    for which in range(1, 1 + ups):

        @pl.loop(1, count)
        def _(step):
            copy(which, step).wait_recv()

    for which in range(1 + ups):

        @pl.loop(1, count)
        def _(step):
            copy(which, step).wait_send()

    for store in stores_out:
        store.wait()


def exchange(owner, x, weights, sends, serves, stores):
    count = serves * stores
    rows = x.shape[0]
    ups = len(sends) - 1
    anywhere = pl.BlockSpec(memory_space=pl.ANY)
    bases = [(rows, w.shape[1]) for w in weights]
    low = jax.ShapeDtypeStruct((rows, stores * RANK), jnp.bfloat16)
    return pl.pallas_call(
        functools.partial(exchange_kernel, serves, stores, ups),
        out_shape=[jax.ShapeDtypeStruct(base, jnp.float32) for base in bases]
        + [low, low]
        + [jax.ShapeDtypeStruct(a.shape, a.dtype) for a in sends[1:]],
        in_specs=[VMEM] + [anywhere] * 4 + [VMEM] * len(sends),
        out_specs=[anywhere] * 3 + [VMEM] * (2 + ups),
        scratch_shapes=[pltpu.VMEM(sends[0].shape, sends[0].dtype), pltpu.VMEM(x.shape, x.dtype)]
        + [pltpu.VMEM(w.shape, w.dtype) for w in weights]
        + [pltpu.VMEM(base, jnp.float32) for base in bases]
        + [
            pltpu.SemaphoreType.DMA((1 + ups, count)),
            pltpu.SemaphoreType.DMA((1 + ups, count)),
            pltpu.SemaphoreType.DMA((4,)),
            pltpu.SemaphoreType.DMA((3,)),
        ],
        compiler_params=pltpu.CompilerParams(
            collective_id=1, has_side_effects=True, vmem_limit_bytes=56 << 20
        ),
        name="exchange",
    )(owner, x, *weights, *sends)


def turned(x, cos, sin):
    lane = lax.broadcasted_iota(jnp.int32, x.shape, 1)
    other = jnp.where(
        lane % HEAD_DIM < HEAD_DIM // 2,
        pltpu.roll(x, LANES - HEAD_DIM // 2, 1),
        pltpu.roll(x, HEAD_DIM // 2, 1),
    )
    return x * cos + other * sin


def columns(ref):
    pieces, stores, rank, width = ref.shape
    parts = [ref[s].reshape(stores * rank, width) for s in range(pieces)]
    return parts[0] if pieces == 1 else jnp.concatenate(parts, axis=1)


def attend_kernel(
    baseq_ref, basek_ref, basev_ref, lowq_ref, lowv_ref, upq_ref, upv_ref, cos_ref, sin_ref, pos_ref, out_ref
):
    rows = baseq_ref.shape[0]
    half = lax.broadcasted_iota(jnp.int32, (rows, LANES), 1) < HEAD_DIM
    cos, sin = cos_ref[...], sin_ref[...]
    delta_q = jnp.dot(lowq_ref[...], columns(upq_ref), preferred_element_type=jnp.float32)
    base = baseq_ref[...] + delta_q.astype(jnp.bfloat16).astype(jnp.float32)
    query = [
        (turned(base[:, p * LANES : (p + 1) * LANES], cos, sin) * HEAD_DIM**-0.5).astype(jnp.bfloat16)
        for p in range(4)
    ]
    keys = turned(basek_ref[...], cos, sin)
    delta_v = jnp.dot(lowv_ref[...], columns(upv_ref), preferred_element_type=jnp.float32)
    values = basev_ref[...] + delta_v.astype(jnp.bfloat16).astype(jnp.float32)

    def split(x):
        left, right = jnp.where(half, x, 0.0), jnp.where(half, 0.0, x)
        return [
            (left.astype(jnp.bfloat16), pltpu.roll(left, HEAD_DIM, 1).astype(jnp.bfloat16)),
            (pltpu.roll(right, HEAD_DIM, 1).astype(jnp.bfloat16), right.astype(jnp.bfloat16)),
        ]

    key_parts, value_parts = split(keys), split(values)
    window = 2 * BLOCK
    ones_half = lax.broadcasted_iota(jnp.int32, (2 * window, LANES), 1) < HEAD_DIM
    ones_top = lax.broadcasted_iota(jnp.int32, (2 * window, LANES), 0) < window
    ones = jnp.where(ones_half == ones_top, 1.0, 0.0).astype(jnp.bfloat16)
    row = lax.broadcasted_iota(jnp.int32, (BLOCK, window), 0)
    col = lax.broadcasted_iota(jnp.int32, (BLOCK, window), 1)
    for b in range(rows // BLOCK):
        first = b * BLOCK
        start = max(0, first - BLOCK)
        here = slice(first, first + BLOCK)
        seen = slice(start, start + window)
        token, key = row + first, col + start
        allowed = (key <= token) & (key >= token - pos_ref[here, :])
        allowed = jnp.concatenate([allowed.astype(jnp.float32)] * 2, axis=0) > 0.5
        for g in range(2):
            kk = jnp.concatenate([part[seen] for part in key_parts[g]], axis=0)
            vv = jnp.concatenate([part[seen] for part in value_parts[g]], axis=0)
            vv = jnp.concatenate([vv, ones], axis=1)
            qq = jnp.concatenate([query[2 * g][here], query[2 * g + 1][here]], axis=0)
            scores = lax.dot_general(qq, kk, CONTRACT_LAST, preferred_element_type=jnp.float32)
            raised = []
            for side in range(2):
                s = jnp.where(allowed, scores[:, side * window : (side + 1) * window], -jnp.inf)
                raised.append(jnp.exp(s - jnp.max(s, axis=1, keepdims=True)))
            weights = jnp.concatenate(raised, axis=1).astype(jnp.bfloat16)
            mixed = jnp.dot(weights, vv, preferred_element_type=jnp.float32)
            done = (mixed[:, :LANES] / mixed[:, LANES:]).astype(jnp.bfloat16)
            for p in range(2):
                at = (2 * g + p) * LANES
                out_ref[here, at : at + LANES] = done[p * BLOCK : (p + 1) * BLOCK]


def up_spec(up, width, skip, cols):
    _, stores, rank, _ = up.shape
    if width >= cols:
        per, off = width // cols, skip // cols
        return pl.BlockSpec((1, stores, rank, cols), lambda j: (j // per, 0, 0, off + j % per))
    return pl.BlockSpec((cols // width, stores, rank, width), lambda j: (j, 0, 0, 0))


def attend(baseq, basek, basev, lowq, lowv, upq, upv, cos, sin, pos, serves, joined):
    rows, width = baseq.shape
    steps = basek.shape[1] // LANES
    wide = width // steps

    def block(cols):
        return pl.BlockSpec((rows, cols), lambda j: (0, j))

    def whole(a):
        return pl.BlockSpec(a.shape, lambda j: (0, 0))

    return pl.pallas_call(
        attend_kernel,
        out_shape=jax.ShapeDtypeStruct((rows, width), jnp.bfloat16),
        grid=(steps,),
        in_specs=[
            block(wide),
            block(LANES),
            block(LANES),
            whole(lowq),
            whole(lowv),
            up_spec(upq, width // serves, 0, wide),
            up_spec(upv, basev.shape[1] // serves, width // serves if joined else 0, LANES),
            whole(cos),
            whole(sin),
            whole(pos),
        ],
        out_specs=block(wide),
        compiler_params=pltpu.CompilerParams(vmem_limit_bytes=60 << 20),
        name="attend",
    )(baseq, basek, basev, lowq, lowv, upq, upv, cos, sin, pos)


def local(x, wq, wk, wv, down, upq, upv, panel_slot, adapters, lengths):
    axes = ("serve", "store")
    serves, stores = lax.axis_size("serve"), lax.axis_size("store")
    my_store = lax.axis_index("store")
    rows = x.shape[0]
    per_store = down.shape[0]
    lengths, adapters = lengths[0], adapters[0]
    requests = lengths.shape[0]

    entries = jnp.arange(panel_slot.shape[0], dtype=jnp.int32)
    slots = jnp.sum(jnp.where(adapters[:, None] == entries[None, :], panel_slot[None, :], 0), axis=1)
    owners = slots // per_store
    store_ids = jnp.arange(stores, dtype=jnp.int32)
    asked = jnp.sum(
        jnp.where(owners[None, :] == store_ids[:, None], slots[None, :] % per_store, 0), axis=1
    )
    row = jnp.pad(asked, (0, LANES - stores))[None, :]
    all_asked = ask(row, serves, stores)[:, 0, :]
    lanes = jnp.arange(LANES, dtype=jnp.int32)
    pick = jnp.sum(jnp.where(lanes[None, :] == my_store, all_asked, 0), axis=1)
    joined = upv.shape[2] % LANES == 0

    sends = choose(pick, down, upq, upv, joined)

    order = jnp.arange(requests, dtype=jnp.int32)
    ends = jnp.sum(jnp.where(order[None, :] <= order[:, None], lengths[None, :], 0), axis=1)
    token = jnp.arange(rows, dtype=jnp.int32)
    member = (token[:, None] < ends[None, :]) & (token[:, None] >= (ends - lengths)[None, :])
    positions = token - jnp.sum(jnp.where(member, (ends - lengths)[None, :], 0), axis=1)
    owner = jnp.sum(jnp.where(member, owners[None, :], 0), axis=1)
    frequency = 500000.0 ** (
        -(jnp.arange(HEAD_DIM // 2).astype(jnp.float32) * 2.0 / HEAD_DIM)
    )
    angles = positions.astype(jnp.float32)[:, None] * frequency[None, :]
    cos, sin = jnp.cos(angles), jnp.sin(angles)
    cos = jnp.concatenate([cos] * 4, axis=1)
    sin = jnp.concatenate([-sin, sin] * 2, axis=1)
    pos = jnp.broadcast_to(positions[:, None], (rows, LANES))
    owner = jnp.broadcast_to(owner[:, None], (rows, LANES))

    baseq, basek, basev, lowq, lowv, *up_got = exchange(
        owner, x, (wq, wk, wv), sends, serves, stores
    )
    up_got = [a.reshape((serves, stores) + a.shape[1:]) for a in up_got]
    upq_got, upv_got = up_got[0], up_got[-1]
    return attend(baseq, basek, basev, lowq, lowv, upq_got, upv_got, cos, sin, pos, serves, joined)


def solution(mesh):
    both = P(("serve", "store"), None)
    panel = P("store", None, "serve")
    return jax.shard_map(
        local,
        mesh=mesh,
        in_specs=(both, P(), P(), P(), panel, panel, panel, P(), both, both),
        out_specs=both,
        check_vma=False,
    )
```
